256 devices in a mesh: inner: 32 (over z_lo, y, core), outer: 8 (over x, z_hi).
Axes of the slice: x: 4, y: 4, z: 8 (z_hi: 2, z_lo: 4; z = z_hi * 4 + z_lo), core: 2. Of those that a mesh axis runs over, the one named last changes fastest.
Arguments:
- activations: bfloat16 [65536, 512], P(('inner', 'outer')), may hold values from -12 to 12
- cotangent: bfloat16 [65536, 14336], P(('inner', 'outer')), may hold values from -0.046875 to 0.046875
Outputs:
- weight_grad: float32 [512, 14336], P(('inner', 'outer'))
The draws below stay inside these ranges and needn't reach their ends.
All inputs are finite; a program needn't handle non-finite values.
Results may differ from the reference program's by a relative error of at most 0.014.
Values may be sent and summed in bfloat16 or wider, within the bound.
A program may use at most 192 MiB of HBM per device.

```python
import math
import jax
import jax.numpy as jnp
from jax import lax

TOK_DEV = 256
GROWS = 512
GCOLS = 14336
TOKENS = 65536
N_INNER = 32
N_OUTER = 8


def scaled_columns(scale_key, value_key, rows, columns, scale_lo, scale_hi, value_bound):
    scales = jnp.exp(jax.random.uniform(scale_key, (columns,), jnp.float32, math.log(scale_lo), math.log(scale_hi)))
    normal_values = jax.random.truncated_normal(value_key, -value_bound, value_bound, (rows, columns), jnp.float32)
    values = normal_values
    return values * scales[None, :]


def draw_activations(key, part):
    key = jax.random.fold_in(key, 11)
    scale_key, value_key = jax.random.split(key)
    values = scaled_columns(scale_key, value_key, TOKENS, GROWS, 0.3, 3.0, 4.0)
    return values.astype(jnp.bfloat16)


def draw_cotangent(key, part):
    key = jax.random.fold_in(key, 12)
    scale_key, value_key = jax.random.split(key)
    norm_factor = 0.99 / math.sqrt(TOKENS)
    values = scaled_columns(scale_key, value_key, TOKENS, GCOLS, 0.3, 3.0, 4.0)
    return (values * norm_factor).astype(jnp.bfloat16)


def setup_inputs(seed: int = 0) -> dict:
    splits = jax.random.split(jax.random.key(seed), 3)
    return {
        "activations": draw_activations(jax.random.fold_in(splits[2], 71), 0),
        "cotangent": draw_cotangent(jax.random.fold_in(splits[2], 71), 0),
    }


epsilon = 1e-06
code_range = 448.0
clip_ratio = 2.0

def hadamard():
    indices = jnp.arange(128, dtype=jnp.int32)
    common_bits = indices[:, None] & indices[None, :]
    bit_count = jnp.zeros((128, 128), jnp.int32)
    for shift_by in range(7):
        bit_count = bit_count + (common_bits >> shift_by & 1)
    signs = 1 - 2 * (bit_count % 2)
    return signs.astype(jnp.float32) / math.sqrt(128.0)

def rotate(blocks, hadamard_matrix):
    return jnp.einsum('rbk,kj->rbj', blocks, hadamard_matrix, precision=lax.Precision.HIGHEST)

def quantize(blocks):
    mean_square = lax.optimization_barrier(jnp.mean(blocks * blocks, axis=-1))
    block_scale = clip_ratio * jnp.sqrt(mean_square + epsilon) / code_range
    coded = jnp.clip(blocks / block_scale[..., None], -code_range, code_range).astype(jnp.bfloat16)
    return (coded, block_scale)

def dequantize(coded, block_scale):
    return coded.astype(jnp.float32) * block_scale[..., None]

def reference(activations, cotangent):
    hadamard_matrix = hadamard()
    block_count = GCOLS // 128
    act_blocks = activations.reshape(N_INNER, N_OUTER, TOK_DEV, GROWS)
    cot_blocks = cotangent.reshape(N_INNER, N_OUTER, TOK_DEV, GCOLS)

    def device_term(act_rows, cot_rows):
        local_grad = lax.dot_general(act_rows, cot_rows, (((0,), (0,)), ((), ())), preferred_element_type=jnp.float32)
        coded, block_scale = quantize(rotate(local_grad.reshape(GROWS, block_count, 128), hadamard_matrix))
        return dequantize(coded, block_scale)

    def outer_step(running, outer_index):

        def inner_step(partial_value, inner_index):
            return (partial_value + device_term(act_blocks[inner_index, outer_index], cot_blocks[inner_index, outer_index]), None)
        partial_value, _ = lax.scan(inner_step, jnp.zeros((GROWS, block_count, 128), jnp.float32), jnp.arange(N_INNER))
        coded, block_scale = quantize(partial_value)
        return (running + dequantize(coded, block_scale), None)
    summed, _ = lax.scan(outer_step, jnp.zeros((GROWS, block_count, 128), jnp.float32), jnp.arange(N_OUTER))
    return rotate(summed, hadamard_matrix).reshape(GROWS, GCOLS)
```

```python
import functools

import jax
import jax.numpy as jnp
from jax import lax
from jax.experimental import pallas as pl
from jax.experimental.pallas import tpu as pltpu
from jax.sharding import PartitionSpec as P

MESH = pl.DeviceIdType.MESH
epsilon = 1e-06
LANES = 128
y_jobs, y_width = 12, 4
z_jobs, z_width = 4, 2
round_blocks = 8
y_per_round = round_blocks // y_width
y_rounds = y_jobs * y_width // round_blocks
rounds = y_rounds + z_jobs * z_width // round_blocks
half_blocks = y_jobs * y_width + z_jobs * z_width
half_cols = half_blocks * LANES
WY, WZ = y_width * LANES, z_width * LANES
TOK, ROWS = 256, 512
f32, bf16 = jnp.float32, jnp.bfloat16


def near(v):
    return v + 1 - 2 * (v % 2)


def signs():
    r = lax.broadcasted_iota(jnp.int32, (256, 256), 0)
    q = lax.broadcasted_iota(jnp.int32, (256, 256), 1)
    common = r & q & 127
    common = common ^ (common >> 4)
    common = common ^ (common >> 2)
    common = common ^ (common >> 1)
    sign = (1 - 2 * (common & 1)).astype(f32)
    return jnp.where((r >> 7) == (q >> 7), sign, 0.0).astype(bf16)


def clipped(v):
    total = jnp.sum(v * v, axis=-1, keepdims=True)
    four = total * (4.0 / LANES) + 4.0 * LANES * epsilon
    bound = four * lax.rsqrt(four)
    return jnp.minimum(jnp.maximum(v, -bound), bound)


def kernel(act, cot, out, h2, at2, asib, cy_own, cy_sib, cz_own, cz_sib, ch, ty, tz,
           ry1a, ry1b, ry2a, ry2b, ry3, ry4, rz1, rz2, rz3a, rz3b, rz4a, rz4b,
           part_y, part_z, coded, arrived,
           s_loc, s_a, s_cot, s_y1, s_y2, s_y3, s_y4, s_z1, s_z2, s_z3, s_z4, s_out):
    i, o = lax.axis_index("inner"), lax.axis_index("outer")
    z, y, c = i // 8, (i // 2) % 4, i % 2
    yn, yf, yo = near(y), 3 - y, (y + 2) % 4
    zn, zf, zo = near(z), 3 - z, (z + 2) % 4

    def dev(z_, y_, c_, o_):
        return (z_ * 8 + y_ * 2 + c_, o_)

    sib = dev(z, y, 1 - c, o)
    dev_yn, dev_yf = dev(z, yn, c, o), dev(z, yf, c, o)
    dev_zn, dev_zf = dev(zn, y, c, o), dev(zf, y, c, o)
    mine = c * 8 + o

    def other(d):
        at = (mine + d) % 16
        return at, dev(z, y, at // 8, at % 8)

    def send(src, dst, sems, where, to):
        return pltpu.make_async_remote_copy(
            src_ref=src, dst_ref=dst, send_sem=sems.at[(0,) + where], recv_sem=sems.at[(1,) + where],
            device_id=to, device_id_type=MESH)

    barrier = pltpu.get_barrier_semaphore()

    def greet(d, _):
        pl.semaphore_signal(barrier, inc=1, device_id=other(d)[1], device_id_type=MESH)
        return 0

    for to in (dev_yn, dev_yf, dev_zn, dev_zf):
        pl.semaphore_signal(barrier, inc=1, device_id=to, device_id_type=MESH)
    lax.fori_loop(1, 16, greet, 0)

    def y_cols(half, j):
        return pl.ds(pl.multiple_of(half * half_cols + j * WY, LANES), WY)

    def z_cols(half, j):
        return pl.ds(pl.multiple_of(half * half_cols + y_jobs * WY + j * WZ, LANES), WZ)

    def load_y(j):
        return pltpu.make_async_copy(cot.at[:, y_cols(c, j)], cy_own.at[j], s_loc.at[j])

    def load_z(j):
        return pltpu.make_async_copy(cot.at[:, z_cols(c, j)], cz_own.at[j], s_loc.at[y_jobs + j])

    def lend_y(j):
        return send(cot.at[:, y_cols(1 - c, j)], cy_sib.at[j], s_cot, (j,), sib)

    def lend_z(j):
        return send(cot.at[:, z_cols(1 - c, j)], cz_sib.at[j], s_cot, (y_jobs + j,), sib)

    def each(n, f):
        def step(j, _):
            f(j)
            return 0
        lax.fori_loop(0, n, step, 0)

    def start_loads(j):
        load_y(j).start()

        @pl.when(j < z_jobs)
        def _():
            load_z(j).start()

    def start_lends(j):
        lend_y(j).start()

        @pl.when(j < z_jobs)
        def _():
            lend_z(j).start()

    each(y_jobs, start_loads)
    h2[...] = signs()

    def turn(which, a):
        t = a.astype(f32).T.astype(bf16)
        at2[which, :, 0:TOK] = t
        at2[which, :, TOK:2 * TOK] = t

    turn(0, act[...])
    pl.semaphore_wait(barrier, 19)
    lend_a = send(act, asib, s_a, (), sib)
    lend_a.start()
    each(y_jobs, start_lends)
    lend_a.wait_recv()
    turn(1, asib[...])

    def compute(own, other_, t, width):
        for which, block in ((0, own), (1, other_)):
            for p in range(width // 256):
                cols = slice(p * 256, p * 256 + 256)
                v = jnp.dot(block[:, cols], h2[...], preferred_element_type=f32)
                hi = v.astype(bf16)
                ch[which, 0:TOK, cols] = hi
                ch[which, TOK:2 * TOK, cols] = (v - hi.astype(f32)).astype(bf16)

        def rows(q, _):
            at = pl.ds(pl.multiple_of(q * 256, 256), 256)
            for p in range(width // 256):
                cols = slice(p * 256, p * 256 + 256)
                a = jnp.dot(at2[0, at, :], ch[0, :, cols], preferred_element_type=f32)
                b = jnp.dot(at2[1, at, :], ch[1, :, cols], preferred_element_type=f32)
                for k in range(2):
                    lanes = slice(k * LANES, k * LANES + LANES)
                    s = (clipped(a[:, lanes]) + clipped(b[:, lanes])).astype(bf16)
                    to = slice(p * 256 + k * LANES, p * 256 + k * LANES + LANES)
                    for zz in range(2):
                        for yy in range(4):
                            t[yy, q * 2 + zz, :, to] = s[zz * 128 + yy * 32:zz * 128 + yy * 32 + 32]
            return 0

        lax.fori_loop(0, 2, rows, 0)

    lo, hi_ = pl.ds(0, 2), pl.ds(2, 2)

    def y1(j):
        return (send(ty.at[j, yo, lo], ry1a.at[j, 1], s_y1, (j, 0), dev_yn),
                send(ty.at[j, yo, hi_], ry1b.at[j, 1], s_y1, (j, 1), dev_yf),
                send(ty.at[j, yn, lo], ry1a.at[j, 0], s_y1, (j, 2), dev_yn),
                send(ty.at[j, yf, hi_], ry1b.at[j, 0], s_y1, (j, 3), dev_yf))

    def y2(j):
        return (send(ty.at[j, yf, lo], ry2a.at[j], s_y2, (j, 0), dev_yf),
                send(ty.at[j, yn, hi_], ry2b.at[j], s_y2, (j, 1), dev_yn))

    def y3(j):
        return (send(ty.at[j, y, zo], ry3.at[j, 1], s_y3, (j, 0), dev_zn),
                send(ty.at[j, y, zn], ry3.at[j, 0], s_y3, (j, 1), dev_zn))

    def y4(j):
        return (send(ty.at[j, y, zf], ry4.at[j], s_y4, (j,), dev_zf),)

    def start(copies):
        for cp in copies:
            cp.start()

    def y_stage0(j):
        load_y(j).wait()
        lend_y(j).wait_recv()
        compute(cy_own.at[j], cy_sib.at[j], ty.at[j], WY)
        start(y1(j))

    def y_stage1(j):
        first_a, first_b, last_a, last_b = y1(j)
        second_a, second_b = y2(j)
        first_a.wait_recv()
        ty[j, yf, 0:2] = ty[j, yf, 0:2] + ry1a[j, 1]
        second_a.start()
        first_b.wait_recv()
        ty[j, yn, 2:4] = ty[j, yn, 2:4] + ry1b[j, 1]
        second_b.start()
        last_a.wait_recv()
        ty[j, y, 0:2] = ty[j, y, 0:2] + ry1a[j, 0]
        last_b.wait_recv()
        ty[j, y, 2:4] = ty[j, y, 2:4] + ry1b[j, 0]

    def y_stage2(j):
        a, b = y2(j)
        a.wait_recv()
        ty[j, y, 0:2] = ty[j, y, 0:2] + ry2a[j]
        b.wait_recv()
        ty[j, y, 2:4] = ty[j, y, 2:4] + ry2b[j]
        start(y3(j))

    def y_stage3(j):
        first, last = y3(j)
        first.wait_recv()
        ty[j, y, zf] = ty[j, y, zf] + ry3[j, 1]
        start(y4(j))
        last.wait_recv()
        ty[j, y, z] = ty[j, y, z] + ry3[j, 0]

    def out_copy(g, d):
        at, to = other(d)
        return send(coded.at[g, at], arrived.at[g, mine], s_out, (g, d), to)

    def send_round(g, part):
        for d in range(16):
            rows = [part[pl.ds(2 * d + e, round_blocks, stride=32), :] for e in range(2)]
            coded[g, d] = jnp.concatenate(rows, axis=0).astype(bf16)

        def go(d, _):
            out_copy(g, d).start()
            return 0

        lax.fori_loop(1, 16, go, 0)
        arrived[g, mine] = coded[g, mine]

    def y_stage4(j):
        y4(j)[0].wait_recv()
        v = ty[j, y, z].astype(f32) + ry4[j].astype(f32)
        for k in range(y_width):
            to = pl.multiple_of((j % y_per_round) * (y_width * 32) + k * 32, 32)
            part_y[pl.ds(to, 32), :] = clipped(v[:, k * LANES:(k + 1) * LANES])

        @pl.when(j % y_per_round == y_per_round - 1)
        def _():
            send_round(j // y_per_round, part_y)

    top, bottom = pl.ds(0, 16), pl.ds(16, 16)

    def z1(j):
        return (send(tz.at[j, :, zo], rz1.at[j, 1], s_z1, (j, 0), dev_zn),
                send(tz.at[j, :, zn], rz1.at[j, 0], s_z1, (j, 1), dev_zn))

    def z2(j):
        return (send(tz.at[j, :, zf], rz2.at[j], s_z2, (j,), dev_zf),)

    def z3(j):
        return (send(tz.at[j, yo, z, top], rz3a.at[j, 1], s_z3, (j, 0), dev_yn),
                send(tz.at[j, yo, z, bottom], rz3b.at[j, 1], s_z3, (j, 1), dev_yf),
                send(tz.at[j, yn, z, top], rz3a.at[j, 0], s_z3, (j, 2), dev_yn),
                send(tz.at[j, yf, z, bottom], rz3b.at[j, 0], s_z3, (j, 3), dev_yf))

    def z4(j):
        return (send(tz.at[j, yf, z, top], rz4a.at[j], s_z4, (j, 0), dev_yf),
                send(tz.at[j, yn, z, bottom], rz4b.at[j], s_z4, (j, 1), dev_yn))

    def z_stage0(j):
        load_z(j).wait()
        lend_z(j).wait_recv()
        compute(cz_own.at[j], cz_sib.at[j], tz.at[j], WZ)
        start(z1(j))

    def z_stage1(j):
        first, last = z1(j)
        first.wait_recv()
        tz[j, :, zf] = tz[j, :, zf] + rz1[j, 1]
        start(z2(j))
        last.wait_recv()
        tz[j, :, z] = tz[j, :, z] + rz1[j, 0]

    def z_stage2(j):
        z2(j)[0].wait_recv()
        tz[j, :, z] = tz[j, :, z] + rz2[j]
        start(z3(j))

    def z_stage3(j):
        first_a, first_b, last_a, last_b = z3(j)
        second_a, second_b = z4(j)
        first_a.wait_recv()
        tz[j, yf, z, 0:16] = tz[j, yf, z, 0:16] + rz3a[j, 1]
        second_a.start()
        first_b.wait_recv()
        tz[j, yn, z, 16:32] = tz[j, yn, z, 16:32] + rz3b[j, 1]
        second_b.start()
        last_a.wait_recv()
        tz[j, y, z, 0:16] = tz[j, y, z, 0:16] + rz3a[j, 0]
        last_b.wait_recv()
        tz[j, y, z, 16:32] = tz[j, y, z, 16:32] + rz3b[j, 0]

    def z_stage4(j):
        a, b = z4(j)
        a.wait_recv()
        b.wait_recv()
        v = tz[j, y, z].astype(f32)
        v = v + jnp.concatenate([rz4a[j], rz4b[j]], axis=0).astype(f32)
        for k in range(z_width):
            to = pl.multiple_of(j * (z_width * 32) + k * 32, 32)
            part_z[pl.ds(to, 32), :] = clipped(v[:, k * LANES:(k + 1) * LANES])

        @pl.when(j == z_jobs - 1)
        def _():
            send_round(y_rounds, part_z)

    def finish(g):
        def take(d, _):
            out_copy(g, d).wait_recv()
            return 0

        lax.fori_loop(1, 16, take, 0)
        for half in range(2):
            total = arrived[g, half * 8].astype(f32)
            for k in range(1, 8):
                total = total + arrived[g, half * 8 + k].astype(f32)
            hi = total.astype(bf16)
            rest = (total - hi.astype(f32)).astype(bf16)
            h = h2[0:LANES, 0:LANES]
            v = jnp.dot(hi, h, preferred_element_type=f32) + jnp.dot(rest, h, preferred_element_type=f32)
            v = v * (1.0 / LANES)
            to = pl.ds(pl.multiple_of(half * half_blocks + g * round_blocks, 8), round_blocks)
            out[0, to, :] = v[0:8]
            out[1, to, :] = v[8:16]

    def tick(t, _):
        def at(stage, jobs, f):
            @pl.when((t >= stage) & (t < jobs + stage))
            def _():
                f(t - stage)

        at(0, y_jobs, y_stage0)
        at(0, z_jobs, z_stage0)
        at(1, y_jobs, y_stage1)
        at(1, z_jobs, z_stage1)
        at(2, y_jobs, y_stage2)
        at(2, z_jobs, z_stage2)
        at(3, y_jobs, y_stage3)
        at(3, z_jobs, z_stage3)
        at(4, y_jobs, y_stage4)
        at(4, z_jobs, z_stage4)
        return 0

    lax.fori_loop(0, y_jobs + 4, tick, 0)
    finish(y_rounds)
    each(y_rounds, finish)

    lend_a.wait_send()

    def drain_y(j):
        for cp in (lend_y(j),) + y1(j) + y2(j) + y3(j) + y4(j):
            cp.wait_send()

    def drain_z(j):
        for cp in (lend_z(j),) + z1(j) + z2(j) + z3(j) + z4(j):
            cp.wait_send()

    each(y_jobs, drain_y)
    each(z_jobs, drain_z)

    def drain_round(g):
        def gone(d, _):
            out_copy(g, d).wait_send()
            return 0
        lax.fori_loop(1, 16, gone, 0)

    each(rounds, drain_round)


def on_device(activations, cotangent):
    dma = pltpu.SemaphoreType.DMA
    vm = pltpu.VMEM
    ny, nz = y_jobs, z_jobs
    out = pl.pallas_call(
        kernel,
        out_shape=jax.ShapeDtypeStruct((2, 2 * half_blocks, LANES), f32),
        in_specs=[pl.BlockSpec(memory_space=pltpu.VMEM), pl.BlockSpec(memory_space=pl.ANY)],
        out_specs=pl.BlockSpec(memory_space=pltpu.VMEM),
        scratch_shapes=[
            vm((256, 256), bf16),
            vm((2, ROWS, 2 * TOK), bf16),
            vm((TOK, ROWS), bf16),
            vm((ny, TOK, WY), bf16), vm((ny, TOK, WY), bf16),
            vm((nz, TOK, WZ), bf16), vm((nz, TOK, WZ), bf16),
            vm((2, 2 * TOK, max(WY, WZ)), bf16),
            vm((ny, 4, 4, 32, WY), bf16),
            vm((nz, 4, 4, 32, WZ), bf16),
            vm((ny, 2, 2, 32, WY), bf16), vm((ny, 2, 2, 32, WY), bf16),
            vm((ny, 2, 32, WY), bf16), vm((ny, 2, 32, WY), bf16),
            vm((ny, 2, 32, WY), bf16), vm((ny, 32, WY), bf16),
            vm((nz, 2, 4, 32, WZ), bf16), vm((nz, 4, 32, WZ), bf16),
            vm((nz, 2, 16, WZ), bf16), vm((nz, 2, 16, WZ), bf16),
            vm((nz, 16, WZ), bf16), vm((nz, 16, WZ), bf16),
            vm((32 * round_blocks, LANES), f32), vm((32 * round_blocks, LANES), f32),
            vm((rounds, 16, 16, LANES), bf16), vm((rounds, 16, 16, LANES), bf16),
            dma((ny + nz,)), dma((2,)), dma((2, ny + nz)),
            dma((2, ny, 4)), dma((2, ny, 2)), dma((2, ny, 2)), dma((2, ny)),
            dma((2, nz, 2)), dma((2, nz)), dma((2, nz, 4)), dma((2, nz, 2)),
            dma((2, rounds, 16)),
        ],
        compiler_params=pltpu.CompilerParams(
            collective_id=0, has_side_effects=True, vmem_limit_bytes=48 * 1024 * 1024),
        name="reduce_gradient",
    )(activations, cotangent)
    return out.reshape(2, 2 * half_cols)


def solution(mesh):
    placed = (P(("inner", "outer"), None), P(("inner", "outer"), None))
    return jax.shard_map(
        on_device,
        mesh=mesh,
        in_specs=placed,
        out_specs=P(("inner", "outer"), None),
        check_vma=False,
    )
```

```python
import jax
import jax.numpy as jnp
from jax import lax
from jax.experimental import pallas as pl
from jax.experimental.pallas import tpu as pltpu
from jax.sharding import PartitionSpec as P

MESH = pl.DeviceIdType.MESH
epsilon = 1e-06
LANES = 128
y_jobs, y_width = 12, 4
z_jobs, z_width = 4, 2
z_period, x_lag, h_lag = 3, 1, 2
y_at = (0, 1, 2, 3, 4)
z_at = (0, 1, 2, 3, 4)
round_blocks = 8
y_per_round = round_blocks // y_width
y_rounds = y_jobs * y_width // round_blocks
rounds = y_rounds + z_jobs * z_width // round_blocks
half_blocks = y_jobs * y_width + z_jobs * z_width
half_cols = half_blocks * LANES
WY, WZ = y_width * LANES, z_width * LANES
TOK, ROWS = 256, 512
f32, bf16 = jnp.float32, jnp.bfloat16


def near(v):
    return v + 1 - 2 * lax.rem(v, 2)


def place(v, order):
    return jnp.where(v == order[0], 0, jnp.where(v == order[1], 1, jnp.where(v == order[2], 2, 3)))


def signs():
    r = lax.broadcasted_iota(jnp.int32, (256, 256), 0)
    q = lax.broadcasted_iota(jnp.int32, (256, 256), 1)
    common = r & q & 127
    common = common ^ (common >> 4)
    common = common ^ (common >> 2)
    common = common ^ (common >> 1)
    sign = (1 - 2 * (common & 1)).astype(f32)
    return jnp.where((r >> 7) == (q >> 7), sign, 0.0).astype(bf16)


def clipped(v):
    total = jnp.sum(v * v, axis=-1, keepdims=True)
    four = total * (4.0 / LANES) + 4.0 * LANES * epsilon
    bound = four * lax.rsqrt(four)
    return jnp.minimum(jnp.maximum(v, -bound), bound)


def each(n, f):
    def step(j, _):
        f(j)
        return 0
    lax.fori_loop(0, n, step, 0)


def kernel(act, cot, out, h2, at2, aown, asib, cy_own, cy_sib, cz_own, cz_sib, ch, ty, tz,
           ry1, ry2, ry3, ry4, rz1, rz2, rz3, rz4, part_y, part_z, coded_x, got_x, coded_h, got_h,
           s_loc, s_act, s_send, s_a, s_cot, s_y1, s_y2, s_y3, s_y4, s_z1, s_z2, s_z3, s_z4, s_x, s_h):
    i, o = lax.axis_index("inner"), lax.axis_index("outer")
    z, y, c = lax.div(i, 8), lax.rem(lax.div(i, 2), 4), lax.rem(i, 2)
    x, h = lax.div(o, 2), lax.rem(o, 2)
    yn, yf = near(y), 3 - y
    zn, zf = near(z), 3 - z

    def dev(z_, y_, c_, x_, h_):
        return (z_ * 8 + y_ * 2 + c_, x_ * 2 + h_)

    sib = dev(z, y, 1 - c, x, h)
    dev_yn, dev_yf = dev(z, yn, c, x, h), dev(z, yf, c, x, h)
    dev_zn, dev_zf = dev(zn, y, c, x, h), dev(zf, y, c, x, h)
    x_to = [lax.rem(x + d, 4) for d in (1, 2, 3)]
    h_to = [(c, 1 - h), (1 - c, h), (1 - c, 1 - h)]
    dev_x = [dev(z, y, c, to, h) for to in x_to]
    dev_h = [dev(z, y, c_, x, h_) for c_, h_ in h_to]

    barrier = pltpu.get_barrier_semaphore()
    for to in [dev_yn, dev_yf, dev_zn, dev_zf] + dev_x + dev_h:
        pl.semaphore_signal(barrier, inc=1, device_id=to, device_id_type=MESH)

    def send(src, dst, kind, got, to):
        return pltpu.make_async_remote_copy(
            src_ref=src, dst_ref=dst, send_sem=s_send.at[kind], recv_sem=got, device_id=to, device_id_type=MESH)

    def y_cols(half, j):
        return pl.ds(pl.multiple_of(half * half_cols + j * WY, LANES), WY)

    def z_cols(half, j):
        return pl.ds(pl.multiple_of(half * half_cols + y_jobs * WY + j * WZ, LANES), WZ)

    def load_y(j):
        return pltpu.make_async_copy(cot.at[:, y_cols(c, j)], cy_own.at[j], s_loc.at[j])

    def load_z(j):
        return pltpu.make_async_copy(cot.at[:, z_cols(c, j)], cz_own.at[j], s_loc.at[y_jobs + j])

    def lend_y(j):
        return send(cot.at[:, y_cols(1 - c, j)], cy_sib.at[j], 0, s_cot.at[j], sib)

    def lend_z(j):
        return send(cot.at[:, z_cols(1 - c, j)], cz_sib.at[j], 1, s_cot.at[y_jobs + j], sib)

    def start_loads(j):
        load_y(j).start()

        @pl.when(j < z_jobs)
        def _():
            load_z(j).start()

    def start_lends(j):
        lend_y(j).start()

        @pl.when(j < z_jobs)
        def _():
            lend_z(j).start()

    load_a = pltpu.make_async_copy(act, aown, s_act)
    load_a.start()
    each(y_jobs, start_loads)
    lend_a = send(act, asib, 2, s_a.at[0], sib)
    pl.semaphore_wait(barrier, 10)
    lend_a.start()
    each(y_jobs, start_lends)
    h2[...] = signs()

    def turn(which, a):
        t = a.astype(f32).T.astype(bf16)
        at2[which, :, 0:TOK] = t
        at2[which, :, TOK:2 * TOK] = t

    load_a.wait()
    turn(0, aown[...])
    lend_a.wait_recv()
    turn(1, asib[...])

    def rotate(which, block, width):
        for p in range(width // 256):
            cols = slice(p * 256, p * 256 + 256)
            v = jnp.dot(block[:, cols], h2[...], preferred_element_type=f32)
            hi = v.astype(bf16)
            ch[which, 0:TOK, cols] = hi
            ch[which, TOK:2 * TOK, cols] = (v - hi.astype(f32)).astype(bf16)

    def multiply(width, store):
        def rows(q, _):
            at = pl.ds(pl.multiple_of(q * 256, 256), 256)
            for p in range(width // 256):
                cols = slice(p * 256, p * 256 + 256)
                a = jnp.dot(at2[0, at, :], ch[0, :, cols], preferred_element_type=f32)
                b = jnp.dot(at2[1, at, :], ch[1, :, cols], preferred_element_type=f32)
                for k in range(2):
                    lanes = slice(k * LANES, k * LANES + LANES)
                    s = (clipped(a[:, lanes]) + clipped(b[:, lanes])).astype(bf16)
                    to = slice(p * 256 + k * LANES, p * 256 + k * LANES + LANES)
                    for zz in range(2):
                        zr = place(q * 2 + zz, (z, zf, zn))
                        for yy in range(4):
                            store(zr, yy, to, s[zz * 128 + yy * 32:zz * 128 + yy * 32 + 32])
            return 0

        lax.fori_loop(0, 2, rows, 0)

    def y1(j):
        return tuple(send(ty.at[j, k, pl.ds(2, 2)], ry1.at[j, k], 3, s_y1.at[j, k], to)
                     for k, to in enumerate((dev_yn, dev_yf)))

    def y2(j):
        return tuple(send(ty.at[j, k, 1], ry2.at[j, k], 4, s_y2.at[j, k], to)
                     for k, to in enumerate((dev_yf, dev_yn)))

    def y3(j):
        return send(ty.at[j, 1, 0], ry3.at[j], 5, s_y3.at[j], dev_zn)

    def y4(j):
        return send(ty.at[j, 0, 0, 1], ry4.at[j], 6, s_y4.at[j], dev_zf)

    def y_stage0(j):
        load_y(j).wait()
        rotate(0, cy_own.at[j], WY)
        lend_y(j).wait_recv()
        rotate(1, cy_sib.at[j], WY)

        def store(zr, yy, cols, rows):
            k = zr // 2
            yr = jnp.where(k == 0, place(yy, (y, yf, yn)), place(yy, (y, yn, yf)))
            ty[j, k, yr, zr % 2, :, cols] = rows

        multiply(WY, store)
        for cp in y1(j):
            cp.start()

    def y_stage1(j):
        first, second = y1(j), y2(j)
        for k in range(2):
            first[k].wait_recv()
            ty[j, k, 1] = ty[j, k, 1] + ry1[j, k, 1]
            second[k].start()
        for k in range(2):
            ty[j, k, 0] = ty[j, k, 0] + ry1[j, k, 0]

    def y_stage2(j):
        a, b = y2(j)
        b.wait_recv()
        ty[j, 1, 0] = ty[j, 1, 0] + ry2[j, 1]
        y3(j).start()
        a.wait_recv()
        ty[j, 0, 0] = ty[j, 0, 0] + ry2[j, 0]

    def y_stage3(j):
        y3(j).wait_recv()
        ty[j, 0, 0, 1] = ty[j, 0, 0, 1] + ry3[j, 1]
        y4(j).start()
        ty[j, 0, 0, 0] = ty[j, 0, 0, 0] + ry3[j, 0]

    def x_copies(g):
        return [send(coded_x.at[g, x_to[d]], got_x.at[g, d], 7, s_x.at[g], dev_x[d]) for d in range(3)]

    def send_round(g, part):
        for d in range(16):
            rows = [part[pl.ds(2 * d + e, round_blocks, stride=32), :] for e in range(2)]
            coded_x[g, (d % 8) // 2, d // 8, d % 2] = jnp.concatenate(rows, axis=0).astype(bf16)
        for cp in x_copies(g):
            cp.start()

    def y_stage4(j):
        y4(j).wait_recv()
        v = ty[j, 0, 0, 0].astype(f32) + ry4[j].astype(f32)
        for k in range(y_width):
            to = pl.multiple_of(lax.rem(j, y_per_round) * (y_width * 32) + k * 32, 32)
            part_y[pl.ds(to, 32), :] = clipped(v[:, k * LANES:(k + 1) * LANES])

        @pl.when(lax.rem(j, y_per_round) == y_per_round - 1)
        def _():
            send_round(lax.div(j, y_per_round), part_y)

    def z1(j):
        return send(tz.at[j, pl.ds(2, 2)], rz1.at[j], 8, s_z1.at[j], dev_zn)

    def z2(j):
        return send(tz.at[j, 1], rz2.at[j], 9, s_z2.at[j], dev_zf)

    def z3(j):
        return tuple(send(tz.at[j, 0, k, pl.ds(2, 2)], rz3.at[j, k], 10, s_z3.at[j, k], to)
                     for k, to in enumerate((dev_yn, dev_yf)))

    def z4(j):
        return tuple(send(tz.at[j, 0, k, 1], rz4.at[j, k], 11, s_z4.at[j, k], to)
                     for k, to in enumerate((dev_yf, dev_yn)))

    def z_stage0(j):
        load_z(j).wait()
        rotate(0, cz_own.at[j], WZ)
        lend_z(j).wait_recv()
        rotate(1, cz_sib.at[j], WZ)

        def store(zr, yy, cols, rows):
            tz[j, zr, 0, place(yy, (y, yf, yn)), :, cols] = rows[0:16]
            tz[j, zr, 1, place(yy, (y, yn, yf)), :, cols] = rows[16:32]

        multiply(WZ, store)
        z1(j).start()

    def z_stage1(j):
        z1(j).wait_recv()
        tz[j, 1] = tz[j, 1] + rz1[j, 1]
        z2(j).start()
        tz[j, 0] = tz[j, 0] + rz1[j, 0]

    def z_stage2(j):
        z2(j).wait_recv()
        tz[j, 0] = tz[j, 0] + rz2[j]
        for cp in z3(j):
            cp.start()

    def z_stage3(j):
        first, second = z3(j), z4(j)
        for k in range(2):
            first[k].wait_recv()
            tz[j, 0, k, 1] = tz[j, 0, k, 1] + rz3[j, k, 1]
            second[k].start()
        for k in range(2):
            tz[j, 0, k, 0] = tz[j, 0, k, 0] + rz3[j, k, 0]

    def z_stage4(j):
        for k, cp in enumerate(z4(j)):
            cp.wait_recv()
            v = tz[j, 0, k, 0].astype(f32) + rz4[j, k].astype(f32)
            for b in range(z_width):
                to = pl.multiple_of(j * (z_width * 32) + b * 32 + k * 16, 16)
                part_z[pl.ds(to, 16), :] = clipped(v[:, b * LANES:(b + 1) * LANES])

        @pl.when(j == z_jobs - 1)
        def _():
            send_round(y_rounds, part_z)

    def h_copies(g):
        return [send(coded_h.at[g, h_to[d][0] * 2 + h_to[d][1]], got_h.at[g, d], 12, s_h.at[g], dev_h[d])
                for d in range(3)]

    def wait_round(kind, g, got, sem):
        pltpu.make_async_copy(got.at[g], got.at[g], sem.at[g]).wait()

    def sum_x(g):
        wait_round(7, g, got_x, s_x)
        total = coded_x[g, x].astype(f32)
        for d in range(3):
            total = total + got_x[g, d].astype(f32)
        coded_h[g] = total.astype(bf16).reshape(4, 16, LANES)
        for cp in h_copies(g):
            cp.start()

    def finish(g):
        wait_round(12, g, got_h, s_h)
        for half, a, b in ((c, coded_h[g, c * 2 + h], got_h[g, 0]), (1 - c, got_h[g, 1], got_h[g, 2])):
            total = a.astype(f32) + b.astype(f32)
            hi = total.astype(bf16)
            rest = (total - hi.astype(f32)).astype(bf16)
            r = h2[0:LANES, 0:LANES]
            v = jnp.dot(hi, r, preferred_element_type=f32) + jnp.dot(rest, r, preferred_element_type=f32)
            v = v * (1.0 / LANES)
            to = pl.ds(pl.multiple_of(half * half_blocks + g * round_blocks, 8), round_blocks)
            out[0, to, :] = v[0:8]
            out[1, to, :] = v[8:16]

    y_stages = (y_stage0, y_stage1, y_stage2, y_stage3, y_stage4)
    z_stages = (z_stage0, z_stage1, z_stage2, z_stage3, z_stage4)
    y_sent = y_per_round - 1 + y_at[4]
    z_sent = (z_jobs - 1) * z_period + z_at[4]

    def tick(t, _):
        def at(first, period, jobs, f):
            since = t - first

            @pl.when((since >= 0) & (lax.rem(since, period) == 0) & (since < jobs * period))
            def _():
                f(lax.div(since, period))

        for k in range(5):
            at(y_at[k], 1, y_jobs, y_stages[k])
            at(z_at[k], z_period, z_jobs, z_stages[k])
        at(y_sent + x_lag, y_per_round, y_rounds, sum_x)
        at(z_sent + x_lag, 1, 1, lambda g: sum_x(y_rounds))
        at(z_sent + x_lag + h_lag, 1, 1, lambda g: finish(y_rounds))
        at(y_sent + x_lag + h_lag, y_per_round, y_rounds, finish)
        return 0

    lax.fori_loop(0, y_jobs + y_at[4] + x_lag + h_lag, tick, 0)

    for kind, ref in enumerate((cy_sib, cz_sib, asib, ty.at[:, :, pl.ds(2, 2)], ty.at[:, :, 1], ty.at[:, 1, 0],
                                ty.at[:, 0, 0, 1], coded_x.at[:, pl.ds(0, 3)], tz.at[:, pl.ds(2, 2)], tz.at[:, 1],
                                tz.at[:, 0, :, pl.ds(2, 2)], tz.at[:, 0, :, 1], coded_h.at[:, pl.ds(0, 3)])):
        pltpu.make_async_copy(ref, ref, s_send.at[kind]).wait()


def on_device(activations, cotangent):
    dma = pltpu.SemaphoreType.DMA
    vm = pltpu.VMEM
    ny, nz = y_jobs, z_jobs
    out = pl.pallas_call(
        kernel,
        out_shape=jax.ShapeDtypeStruct((2, 2 * half_blocks, LANES), f32),
        in_specs=[pl.BlockSpec(memory_space=pl.ANY)] * 2,
        out_specs=pl.BlockSpec(memory_space=pltpu.VMEM),
        scratch_shapes=[
            vm((256, 256), bf16),
            vm((2, ROWS, 2 * TOK), bf16),
            vm((TOK, ROWS), bf16), vm((TOK, ROWS), bf16),
            vm((ny, TOK, WY), bf16), vm((ny, TOK, WY), bf16),
            vm((nz, TOK, WZ), bf16), vm((nz, TOK, WZ), bf16),
            vm((2, 2 * TOK, max(WY, WZ)), bf16),
            vm((ny, 2, 4, 2, 32, WY), bf16),
            vm((nz, 4, 2, 4, 16, WZ), bf16),
            vm((ny, 2, 2, 2, 32, WY), bf16), vm((ny, 2, 2, 32, WY), bf16),
            vm((ny, 2, 32, WY), bf16), vm((ny, 32, WY), bf16),
            vm((nz, 2, 2, 4, 16, WZ), bf16), vm((nz, 2, 4, 16, WZ), bf16),
            vm((nz, 2, 2, 16, WZ), bf16), vm((nz, 2, 16, WZ), bf16),
            vm((32 * round_blocks, LANES), f32), vm((32 * round_blocks, LANES), f32),
            vm((rounds, 4, 2, 2, 16, LANES), bf16), vm((rounds, 3, 2, 2, 16, LANES), bf16),
            vm((rounds, 4, 16, LANES), bf16), vm((rounds, 3, 16, LANES), bf16),
            dma((ny + nz,)), dma, dma((13,)), dma((1,)), dma((ny + nz,)),
            dma((ny, 2)), dma((ny, 2)), dma((ny,)), dma((ny,)),
            dma((nz,)), dma((nz,)), dma((nz, 2)), dma((nz, 2)),
            dma((rounds,)), dma((rounds,)),
        ],
        compiler_params=pltpu.CompilerParams(
            collective_id=0, has_side_effects=True, vmem_limit_bytes=48 * 1024 * 1024),
        name="reduce_gradient",
    )(activations, cotangent)
    return out.reshape(2, 2 * half_cols)


def solution(mesh):
    placed = (P(("inner", "outer"), None), P(("inner", "outer"), None))
    return jax.shard_map(
        on_device,
        mesh=mesh,
        in_specs=placed,
        out_specs=P(("inner", "outer"), None),
        check_vma=False,
    )
```

```python
import jax
import jax.numpy as jnp
from jax import lax
from jax.experimental import pallas as pl
from jax.experimental.pallas import tpu as pltpu
from jax.sharding import PartitionSpec as P

MESH = pl.DeviceIdType.MESH
epsilon = 1e-06
LANES = 128
y_jobs = ((4, 2), (6, 2), (8, 2), (10, 2), (12, 2), (14, 2), (16, 2), (18, 2), (20, 2), (22, 2), (26, 2))
z_jobs = ((0, 1), (1, 1), (2, 1), (3, 1), (24, 1), (25, 1))
Y0, Y1, Y2, Y3, Y4, Z0, Z1, Z2, Z3, Z4, XS, HS, OUT = range(13)
steps = (
    (Y0, 4), (Z0, 3), (Y0, 3), (Y0, 1), (Z0, 0), (Z1, 3), (Z0, 5), (Y0, 2), (Z0, 1), (Y1, 3), (Z1, 0),
    (Y1, 1), (Y1, 2), (Y0, 0), (Z0, 4), (Y0, 6), (Y2, 1), (Y1, 4), (Y0, 7), (Z1, 1), (Z0, 2), (Z1, 5),
    (Y2, 2), (Y3, 1), (Y0, 5), (Y1, 0), (Y2, 4), (Z1, 2), (Y2, 3), (Y0, 8), (Z2, 1), (Y1, 5), (Y1, 7),
    (Z1, 4), (Y1, 6), (Y2, 0), (Z2, 0), (Y0, 9), (Y3, 4), (Y2, 5), (Y3, 0), (Y1, 8), (Y4, 1), (Y3, 3),
    (Y4, 4), (Y2, 7), (Y3, 2), (Y0, 10), (Y2, 6), (Y3, 5), (Y4, 3), (Y1, 9), (Y2, 8), (Y4, 2), (Y4, 0),
    (Z2, 3), (Y3, 7), (Y3, 6), (Y1, 10), (Z2, 2), (Z2, 5), (Y3, 8), (XS, 2), (Y4, 5), (Y2, 9), (Z2, 4),
    (XS, 3), (Z3, 3), (XS, 1), (Y4, 7), (Z3, 1), (Y2, 10), (Y4, 6), (Z3, 5), (XS, 4), (Y3, 9), (Z3, 4),
    (Z3, 2), (Z4, 3), (Z3, 0), (HS, 3), (Z4, 1), (Y3, 10), (Z4, 4), (Z4, 2), (Z4, 0), (HS, 4), (XS, 0),
    (Y4, 9), (HS, 1), (Y4, 8), (XS, 5), (Z4, 5), (Y4, 10), (XS, 6), (OUT, 3), (HS, 2), (HS, 0), (HS, 5),
    (HS, 6), (OUT, 1), (OUT, 2), (OUT, 0), (OUT, 4), (OUT, 5), (OUT, 6),
)
pairs = 28
z_first = [sum(n for _, n in z_jobs[:j]) for j in range(len(z_jobs))]
rounds = pairs // 4
half_cols = pairs * 256
TOK, ROWS = 256, 512
f32, bf16 = jnp.float32, jnp.bfloat16


def near(v):
    return v + 1 - 2 * lax.rem(v, 2)


def place(v, order):
    return jnp.where(v == order[0], 0, jnp.where(v == order[1], 1, jnp.where(v == order[2], 2, 3)))


def signs():
    r = lax.broadcasted_iota(jnp.int32, (256, 256), 0)
    q = lax.broadcasted_iota(jnp.int32, (256, 256), 1)
    common = r & q & 127
    common = common ^ (common >> 4)
    common = common ^ (common >> 2)
    common = common ^ (common >> 1)
    sign = (1 - 2 * (common & 1)).astype(f32)
    return jnp.where((r >> 7) == (q >> 7), sign, 0.0).astype(bf16)


def clipped(v):
    total = jnp.sum(v * v, axis=-1, keepdims=True)
    four = total * (4.0 / LANES) + 4.0 * LANES * epsilon
    bound = four * lax.rsqrt(four)
    return jnp.minimum(jnp.maximum(v, -bound), bound)


def each(n, f):
    def step(j, _):
        f(j)
        return 0
    lax.fori_loop(0, n, step, 0)


def kernel(act, cot, out, h2, at2, aown, asib, c_own, c_sib, ch, ty, tz,
           ry1, ry2, ry3, ry4, rz1, rz2, rz3, rz4, part, coded_x, got_x, coded_h, got_h,
           s_loc, s_act, s_send, s_a, s_cot, s_y1, s_y2, s_y3, s_y4, s_z1, s_z2, s_z3, s_z4, s_x, s_h):
    i, o = lax.axis_index("inner"), lax.axis_index("outer")
    z, y, c = lax.div(i, 8), lax.rem(lax.div(i, 2), 4), lax.rem(i, 2)
    x, h = lax.div(o, 2), lax.rem(o, 2)
    yn, yf = near(y), 3 - y
    zn, zf = near(z), 3 - z

    def dev(z_, y_, c_, x_, h_):
        return (z_ * 8 + y_ * 2 + c_, x_ * 2 + h_)

    sib = dev(z, y, 1 - c, x, h)
    dev_yn, dev_yf = dev(z, yn, c, x, h), dev(z, yf, c, x, h)
    dev_zn, dev_zf = dev(zn, y, c, x, h), dev(zf, y, c, x, h)
    x_to = [lax.rem(x + d, 4) for d in (1, 2, 3)]
    h_to = [(c, 1 - h), (1 - c, h), (1 - c, 1 - h)]
    dev_x = [dev(z, y, c, to, h) for to in x_to]
    dev_h = [dev(z, y, c_, x, h_) for c_, h_ in h_to]

    barrier = pltpu.get_barrier_semaphore()
    for to in [dev_yn, dev_yf, dev_zn, dev_zf] + dev_x + dev_h:
        pl.semaphore_signal(barrier, inc=1, device_id=to, device_id_type=MESH)

    def send(src, dst, kind, got, to):
        return pltpu.make_async_remote_copy(
            src_ref=src, dst_ref=dst, send_sem=s_send.at[kind], recv_sem=got, device_id=to, device_id_type=MESH)

    def columns(half, p, n):
        return pl.ds(pl.multiple_of(half * half_cols + p * 256, LANES), n * 256)

    def load(p, n):
        return pltpu.make_async_copy(cot.at[:, columns(c, p, n)], c_own.at[:, columns(0, p, n)], s_loc.at[p])

    def lend(p, n):
        return send(cot.at[:, columns(1 - c, p, n)], c_sib.at[:, columns(0, p, n)], 0, s_cot.at[p], sib)

    first_use = [y_jobs[j] if s == Y0 else z_jobs[j] for s, j in steps if s in (Y0, Z0)]
    load_a = pltpu.make_async_copy(act, aown, s_act)
    load_a.start()
    for p, n in first_use:
        load(p, n).start()
    lend_a = send(act, asib, 1, s_a.at[0], sib)
    pl.semaphore_wait(barrier, 10)
    lend_a.start()
    for p, n in first_use:
        lend(p, n).start()
    h2[...] = signs()

    def turn(which, a):
        t = a.astype(f32).T.astype(bf16)
        at2[which, :, 0:TOK] = t
        at2[which, :, TOK:2 * TOK] = t

    load_a.wait()
    turn(0, aown[...])
    lend_a.wait_recv()
    turn(1, asib[...])

    places_z = [place(v, (z, zf, zn)) for v in range(4)]

    def compute(p, n, store):
        for q in range(n):
            for which, block in enumerate((c_own, c_sib)):
                v = jnp.dot(block[:, columns(0, p + q, 1)], h2[...], preferred_element_type=f32)
                hi = v.astype(bf16)
                ch[which, q, 0:TOK, :] = hi
                ch[which, q, TOK:2 * TOK, :] = (v - hi.astype(f32)).astype(bf16)
        for r in range(2):
            at = slice(r * 256, r * 256 + 256)
            for q in range(n):
                a = jnp.dot(at2[0, at, :], ch[0, q], preferred_element_type=f32)
                b = jnp.dot(at2[1, at, :], ch[1, q], preferred_element_type=f32)
                for k in range(2):
                    lanes = slice(k * LANES, k * LANES + LANES)
                    s = (clipped(a[:, lanes]) + clipped(b[:, lanes])).astype(bf16)
                    for zz in range(2):
                        for yy in range(4):
                            store(q, k, places_z[r * 2 + zz], yy, s[zz * 128 + yy * 32:zz * 128 + yy * 32 + 32])

    place_a = [place(v, (y, yf, yn)) for v in range(4)]
    place_b = [place(v, (y, yn, yf)) for v in range(4)]

    def y1(j):
        ps = pl.ds(*y_jobs[j])
        return tuple(send(ty.at[ps, k, pl.ds(2, 2)], ry1.at[ps, k], 2, s_y1.at[j, k], to)
                     for k, to in enumerate((dev_yn, dev_yf)))

    def y2(j):
        ps = pl.ds(*y_jobs[j])
        return tuple(send(ty.at[ps, k, 1], ry2.at[ps, k], 3, s_y2.at[j, k], to)
                     for k, to in enumerate((dev_yf, dev_yn)))

    def y3(j):
        ps = pl.ds(*y_jobs[j])
        return send(ty.at[ps, 1, 0], ry3.at[ps], 4, s_y3.at[j], dev_zn)

    def y4(j):
        ps = pl.ds(*y_jobs[j])
        return send(ty.at[ps, 0, 0, 1], ry4.at[ps], 5, s_y4.at[j], dev_zf)

    def y_compute(p, n):
        def store(q, k, zr, yy, rows):
            second = lax.div(zr, 2)
            yr = jnp.where(second == 0, place_a[yy], place_b[yy])
            ty[p + q, second, yr, lax.rem(zr, 2), :, k * LANES:(k + 1) * LANES] = rows

        compute(p, n, store)

    def y_stage0(j):
        for cp in y1(j):
            cp.start()

    def y_stage1(j):
        ps = pl.ds(*y_jobs[j])
        first, second = y1(j), y2(j)
        for k in range(2):
            first[k].wait_recv()
            ty[ps, k, 1] = ty[ps, k, 1] + ry1[ps, k, 1]
            second[k].start()
        for k in range(2):
            ty[ps, k, 0] = ty[ps, k, 0] + ry1[ps, k, 0]

    def y_stage2(j):
        ps = pl.ds(*y_jobs[j])
        a, b = y2(j)
        b.wait_recv()
        ty[ps, 1, 0] = ty[ps, 1, 0] + ry2[ps, 1]
        y3(j).start()
        a.wait_recv()
        ty[ps, 0, 0] = ty[ps, 0, 0] + ry2[ps, 0]

    def y_stage3(j):
        ps = pl.ds(*y_jobs[j])
        y3(j).wait_recv()
        ty[ps, 0, 0, 1] = ty[ps, 0, 0, 1] + ry3[ps, 1]
        y4(j).start()
        ty[ps, 0, 0, 0] = ty[ps, 0, 0, 0] + ry3[ps, 0]

    def keep_part(p, k, v):
        at = (p % 4 * 2 + k) * 32
        part[p // 4, at:at + 32, :] = clipped(v)

    def y_stage4(j):
        y4(j).wait_recv()
        first, n = y_jobs[j]
        for p in range(first, first + n):
            v = ty[p, 0, 0, 0].astype(f32) + ry4[p].astype(f32)
            for k in range(2):
                keep_part(p, k, v[:, k * LANES:(k + 1) * LANES])

    def zp(j):
        return pl.ds(z_first[j], z_jobs[j][1])

    def z1(j):
        return send(tz.at[zp(j), pl.ds(2, 2)], rz1.at[zp(j)], 6, s_z1.at[j], dev_zn)

    def z2(j):
        return send(tz.at[zp(j), 1], rz2.at[zp(j)], 7, s_z2.at[j], dev_zf)

    def z3(j):
        return tuple(send(tz.at[zp(j), 0, k, pl.ds(2, 2)], rz3.at[zp(j), k], 8, s_z3.at[j, k], to)
                     for k, to in enumerate((dev_yn, dev_yf)))

    def z4(j):
        return tuple(send(tz.at[zp(j), 0, k, 1], rz4.at[zp(j), k], 9, s_z4.at[j, k], to)
                     for k, to in enumerate((dev_yf, dev_yn)))

    def z_compute(m, p, n):
        def store(q, k, zr, yy, rows):
            tz[m + q, zr, k, (place_a, place_b)[k][yy]] = rows

        compute(p, n, store)

    def z_stage0(j):
        z1(j).start()

    def z_stage1(j):
        ps = zp(j)
        z1(j).wait_recv()
        tz[ps, 1] = tz[ps, 1] + rz1[ps, 1]
        z2(j).start()
        tz[ps, 0] = tz[ps, 0] + rz1[ps, 0]

    def z_stage2(j):
        ps = zp(j)
        z2(j).wait_recv()
        tz[ps, 0] = tz[ps, 0] + rz2[ps]
        for cp in z3(j):
            cp.start()

    def z_stage3(j):
        ps = zp(j)
        first, second = z3(j), z4(j)
        for k in range(2):
            first[k].wait_recv()
            tz[ps, 0, k, 1] = tz[ps, 0, k, 1] + rz3[ps, k, 1]
            second[k].start()
        for k in range(2):
            tz[ps, 0, k, 0] = tz[ps, 0, k, 0] + rz3[ps, k, 0]

    def z_stage4(j):
        for k, cp in enumerate(z4(j)):
            cp.wait_recv()
            for q in range(z_jobs[j][1]):
                m = z_first[j] + q
                keep_part(z_jobs[j][0] + q, k, tz[m, 0, k, 0].astype(f32) + rz4[m, k].astype(f32))

    def x_copies(g):
        return [send(coded_x.at[g, x_to[d]], got_x.at[g, d], 10, s_x.at[g], dev_x[d]) for d in range(3)]

    def h_copies(g):
        return [send(coded_h.at[g, h_to[d][0] * 2 + h_to[d][1]], got_h.at[g, d], 11, s_h.at[g], dev_h[d])
                for d in range(3)]

    def send_x(g):
        for d in range(16):
            rows = [part[g, pl.ds(2 * d + e, 8, stride=32), :] for e in range(2)]
            coded_x[g, (d % 8) // 2, d // 8, d % 2] = jnp.concatenate(rows, axis=0).astype(bf16)
        for cp in x_copies(g):
            cp.start()

    def sum_x(g):
        pltpu.make_async_copy(got_x.at[g], got_x.at[g], s_x.at[g]).wait()
        total = coded_x[g, x].astype(f32)
        for d in range(3):
            total = total + got_x[g, d].astype(f32)
        coded_h[g] = total.astype(bf16).reshape(4, 16, LANES)
        for cp in h_copies(g):
            cp.start()

    def finish(g):
        pltpu.make_async_copy(got_h.at[g], got_h.at[g], s_h.at[g]).wait()
        for half, a, b in ((c, coded_h[g, c * 2 + h], got_h[g, 0]), (1 - c, got_h[g, 1], got_h[g, 2])):
            total = a.astype(f32) + b.astype(f32)
            hi = total.astype(bf16)
            rest = (total - hi.astype(f32)).astype(bf16)
            r = h2[0:LANES, 0:LANES]
            v = jnp.dot(hi, r, preferred_element_type=f32) + jnp.dot(rest, r, preferred_element_type=f32)
            v = v * (1.0 / LANES)
            to = pl.ds(pl.multiple_of(half * (2 * pairs) + g * 8, 8), 8)
            out[0, to, :] = v[0:8]
            out[1, to, :] = v[8:16]

    run = (y_stage0, y_stage1, y_stage2, y_stage3, y_stage4, z_stage0, z_stage1, z_stage2, z_stage3, z_stage4,
           send_x, sum_x, finish)
    starts = [k for k, (stage, _) in enumerate(steps) if stage in (Y0, Z0)] + [len(steps)]
    assert starts[0] == 0
    turns = len(starts) - 1
    sort = [(0 if steps[k][0] == Y0 else 2) + (2 - n) for k, (_, n) in zip(starts, first_use)]
    place_of = [z_first[steps[k][1]] if steps[k][0] == Z0 else 0 for k in starts[:-1]]

    def pick(t, values):
        at = jnp.int32(values[0])
        for k, v in enumerate(values):
            if v != values[0]:
                at = jnp.where(t == k, v, at)
        return at

    def inputs(k):
        load(*first_use[k]).wait()
        lend(*first_use[k]).wait_recv()

    def turn_of(t):
        first, now, m = pick(t, [p for p, _ in first_use]), pick(t, sort), pick(t, place_of)
        for kind in sorted(set(sort)):
            @pl.when(now == kind)
            def _():
                if kind < 2:
                    y_compute(first, 2 - kind)
                else:
                    z_compute(m, first, 4 - kind)

        def among(a, b):
            if b - a > 1:
                mid = (a + b) // 2
                pl.when(t < mid)(lambda: among(a, mid))
                pl.when(t >= mid)(lambda: among(mid, b))
                return
            for stage, j in steps[starts[a]:starts[b]]:
                run[stage](j)
            if b < turns:
                inputs(b)

        among(0, turns)

    inputs(0)
    each(turns, turn_of)

    once = [(0, c_sib), (1, asib), (6, tz.at[:, pl.ds(2, 2)]), (7, tz.at[:, 1]), (8, tz.at[:, 0, :, pl.ds(2, 2)]),
            (9, tz.at[:, 0, :, 1]), (10, coded_x.at[:, pl.ds(0, 3)]), (11, coded_h.at[:, pl.ds(0, 3)])]
    ny = sum(n for _, n in y_jobs)
    once += [(2, ty.at[0:ny, :, pl.ds(2, 2)]), (3, ty.at[0:ny, :, 1]), (4, ty.at[0:ny, 1, 0]),
             (5, ty.at[0:ny, 0, 0, 1])]
    for kind, ref in once:
        pltpu.make_async_copy(ref, ref, s_send.at[kind]).wait()


def on_device(activations, cotangent):
    dma = pltpu.SemaphoreType.DMA
    vm = pltpu.VMEM
    ny, nz = len(y_jobs), len(z_jobs)
    nzp = sum(n for _, n in z_jobs)
    out = pl.pallas_call(
        kernel,
        out_shape=jax.ShapeDtypeStruct((2, 4 * pairs, LANES), f32),
        in_specs=[pl.BlockSpec(memory_space=pl.ANY)] * 2,
        out_specs=pl.BlockSpec(memory_space=pltpu.VMEM),
        scratch_shapes=[
            vm((256, 256), bf16),
            vm((2, ROWS, 2 * TOK), bf16),
            vm((TOK, ROWS), bf16), vm((TOK, ROWS), bf16),
            vm((TOK, half_cols), bf16), vm((TOK, half_cols), bf16),
            vm((2, 2, 2 * TOK, 256), bf16),
            vm((pairs, 2, 4, 2, 32, 256), bf16),
            vm((nzp, 4, 2, 4, 32, LANES), bf16),
            vm((pairs, 2, 2, 2, 32, 256), bf16), vm((pairs, 2, 2, 32, 256), bf16),
            vm((pairs, 2, 32, 256), bf16), vm((pairs, 32, 256), bf16),
            vm((nzp, 2, 2, 4, 32, LANES), bf16), vm((nzp, 2, 4, 32, LANES), bf16),
            vm((nzp, 2, 2, 32, LANES), bf16), vm((nzp, 2, 32, LANES), bf16),
            vm((rounds, 256, LANES), f32),
            vm((rounds, 4, 2, 2, 16, LANES), bf16), vm((rounds, 3, 2, 2, 16, LANES), bf16),
            vm((rounds, 4, 16, LANES), bf16), vm((rounds, 3, 16, LANES), bf16),
            dma((pairs,)), dma, dma((12,)), dma((1,)), dma((pairs,)),
            dma((ny, 2)), dma((ny, 2)), dma((ny,)), dma((ny,)),
            dma((nz,)), dma((nz,)), dma((nz, 2)), dma((nz, 2)),
            dma((rounds,)), dma((rounds,)),
        ],
        compiler_params=pltpu.CompilerParams(
            collective_id=0, has_side_effects=True, vmem_limit_bytes=48 * 1024 * 1024),
        name="reduce_gradient",
    )(activations, cotangent)
    return out.reshape(2, 2 * half_cols)


def solution(mesh):
    placed = (P(("inner", "outer"), None), P(("inner", "outer"), None))
    return jax.shard_map(
        on_device,
        mesh=mesh,
        in_specs=placed,
        out_specs=P(("inner", "outer"), None),
        check_vma=False,
    )
```

```python
import jax
import jax.numpy as jnp
from jax import lax
from jax.experimental import pallas as pl
from jax.experimental.pallas import tpu as pltpu
from jax.sharding import PartitionSpec as P

MESH = pl.DeviceIdType.MESH
epsilon = 1e-06
LANES = 128
y_jobs = ((4, 2), (6, 2), (8, 2), (10, 2), (12, 2), (14, 2), (16, 2), (18, 2), (20, 2), (22, 2), (26, 2))
z_jobs = ((0, 1), (1, 1), (2, 1), (3, 1), (24, 1), (25, 1))
Y0, Y1, Y2, Y3, Y4, Z0, Z1, Z2, Z3, Z4, XS, HS, OUT = range(13)
steps = (
    (Y0, 0), (Z0, 2), (Y0, 1), (Z0, 1), (Y0, 2), (Z0, 3), (Y1, 0), (Y0, 4), (Z0, 4), (Z1, 1), (Y1, 1),
    (Z0, 0), (Z1, 3), (Y2, 0), (Y1, 2), (Y0, 3), (Y0, 5), (Y1, 4), (Z1, 0), (Y2, 2), (Y0, 8), (Y1, 3),
    (Y3, 0), (Y2, 1), (Y0, 7), (Z1, 2), (Y0, 6), (Y2, 4), (Y1, 5), (Z2, 3), (Y3, 1), (Y2, 3), (Y3, 2),
    (Z1, 4), (Z0, 5), (Y3, 4), (Y1, 7), (Y3, 3), (Y0, 9), (Y1, 8), (Y1, 6), (Y0, 10), (Y2, 5), (Y4, 0),
    (Y4, 1), (Z2, 0), (Z1, 5), (Y1, 9), (Z2, 2), (Y2, 7), (Y3, 5), (Z2, 1), (Y4, 2), (Y4, 4), (XS, 1),
    (Y2, 6), (Y3, 7), (Y4, 3), (Y2, 8), (Y1, 10), (Y3, 6), (Z2, 4), (Z3, 0), (Z3, 3), (Y2, 9), (Z2, 5),
    (Y3, 8), (Y4, 7), (Z3, 1), (Y2, 10), (Y4, 5), (Z3, 2), (Z4, 0), (Z4, 3), (Z3, 5), (Y3, 9), (XS, 2),
    (Z3, 4), (Y4, 6), (HS, 1), (Z4, 1), (Z4, 2), (Y3, 10), (Z4, 5), (Y4, 8), (XS, 0), (XS, 4), (Y4, 9),
    (XS, 5), (Z4, 4), (HS, 2), (XS, 3), (Y4, 10), (XS, 6), (OUT, 1), (HS, 0), (HS, 4), (HS, 3), (HS, 5),
    (HS, 6), (OUT, 0), (OUT, 2), (OUT, 4), (OUT, 3), (OUT, 5), (OUT, 6),
)
pairs = 28
z_first = [sum(n for _, n in z_jobs[:j]) for j in range(len(z_jobs))]
rounds = pairs // 4
half_cols = pairs * 256
TOK, ROWS = 256, 512
f32, bf16 = jnp.float32, jnp.bfloat16


def near(v):
    return v + 1 - 2 * lax.rem(v, 2)


def place(v, order):
    return jnp.where(v == order[0], 0, jnp.where(v == order[1], 1, jnp.where(v == order[2], 2, 3)))


def signs():
    r = lax.broadcasted_iota(jnp.int32, (256, 256), 0)
    q = lax.broadcasted_iota(jnp.int32, (256, 256), 1)
    common = r & q & 127
    common = common ^ (common >> 4)
    common = common ^ (common >> 2)
    common = common ^ (common >> 1)
    sign = (1 - 2 * (common & 1)).astype(f32)
    return jnp.where((r >> 7) == (q >> 7), sign, 0.0).astype(bf16)


def clipped(v):
    total = jnp.sum(v * v, axis=-1, keepdims=True)
    four = total * (4.0 / LANES) + 4.0 * LANES * epsilon
    bound = four * lax.rsqrt(four)
    return jnp.minimum(jnp.maximum(v, -bound), bound)


def each(n, f):
    def step(j, _):
        f(j)
        return 0
    lax.fori_loop(0, n, step, 0)


def kernel(act, cot, out, h2, at2, aown, asib, c_own, c_sib, ch, ty, tz,
           ry1, ry2, ry3, ry4, rz1, rz2, rz3, rz4, part, coded_x, got_x, coded_h, got_h,
           s_loc, s_act, s_send, s_a, s_cot, s_y1, s_y2, s_y3, s_y4, s_z1, s_z2, s_z3, s_z4, s_x, s_h):
    i, o = lax.axis_index("inner"), lax.axis_index("outer")
    z, y, c = lax.div(i, 8), lax.rem(lax.div(i, 2), 4), lax.rem(i, 2)
    x, h = lax.div(o, 2), lax.rem(o, 2)
    yn, yf = near(y), 3 - y
    zn, zf = near(z), 3 - z

    def dev(z_, y_, c_, x_, h_):
        return (z_ * 8 + y_ * 2 + c_, x_ * 2 + h_)

    sib = dev(z, y, 1 - c, x, h)
    dev_yn, dev_yf = dev(z, yn, c, x, h), dev(z, yf, c, x, h)
    dev_zn, dev_zf = dev(zn, y, c, x, h), dev(zf, y, c, x, h)
    x_to = [lax.rem(x + d, 4) for d in (1, 2, 3)]
    h_to = [(c, 1 - h), (1 - c, h), (1 - c, 1 - h)]
    dev_x = [dev(z, y, c, to, h) for to in x_to]
    dev_h = [dev(z, y, c_, x, h_) for c_, h_ in h_to]

    barrier = pltpu.get_barrier_semaphore()
    for to in [dev_yn, dev_yf, dev_zn, dev_zf] + dev_x + dev_h:
        pl.semaphore_signal(barrier, inc=1, device_id=to, device_id_type=MESH)

    def send(src, dst, kind, got, to):
        return pltpu.make_async_remote_copy(
            src_ref=src, dst_ref=dst, send_sem=s_send.at[kind], recv_sem=got, device_id=to, device_id_type=MESH)

    def columns(half, p, n):
        return pl.ds(pl.multiple_of(half * half_cols + p * 256, LANES), n * 256)

    def load(p, n):
        return pltpu.make_async_copy(cot.at[:, columns(c, p, n)], c_own.at[:, columns(0, p, n)], s_loc.at[p])

    def lend(p, n):
        return send(cot.at[:, columns(1 - c, p, n)], c_sib.at[:, columns(0, p, n)], 0, s_cot.at[p], sib)

    first_use = [y_jobs[j] if s == Y0 else z_jobs[j] for s, j in steps if s in (Y0, Z0)]
    load_a = pltpu.make_async_copy(act, aown, s_act)
    load_a.start()
    for p, n in first_use:
        load(p, n).start()
    lend_a = send(act, asib, 1, s_a.at[0], sib)
    pl.semaphore_wait(barrier, 10)
    lend_a.start()
    for p, n in first_use:
        lend(p, n).start()
    h2[...] = signs()

    def turn(which, a):
        t = a.astype(f32).T.astype(bf16)
        at2[which, :, 0:TOK] = t
        at2[which, :, TOK:2 * TOK] = t

    load_a.wait()
    turn(0, aown[...])
    lend_a.wait_recv()
    turn(1, asib[...])

    places_z = [place(v, (z, zf, zn)) for v in range(4)]

    def compute(p, n, store):
        for q in range(n):
            for which, block in enumerate((c_own, c_sib)):
                v = jnp.dot(block[:, columns(0, p + q, 1)], h2[...], preferred_element_type=f32)
                hi = v.astype(bf16)
                ch[which, q, 0:TOK, :] = hi
                ch[which, q, TOK:2 * TOK, :] = (v - hi.astype(f32)).astype(bf16)
        for r in range(2):
            at = slice(r * 256, r * 256 + 256)
            for q in range(n):
                a = jnp.dot(at2[0, at, :], ch[0, q], preferred_element_type=f32)
                b = jnp.dot(at2[1, at, :], ch[1, q], preferred_element_type=f32)
                for k in range(2):
                    lanes = slice(k * LANES, k * LANES + LANES)
                    s = (clipped(a[:, lanes]) + clipped(b[:, lanes])).astype(bf16)
                    for zz in range(2):
                        for yy in range(4):
                            store(q, k, places_z[r * 2 + zz], yy, s[zz * 128 + yy * 32:zz * 128 + yy * 32 + 32])

    place_a = [place(v, (y, yf, yn)) for v in range(4)]
    place_b = [place(v, (y, yn, yf)) for v in range(4)]

    def y1(j):
        ps = pl.ds(*y_jobs[j])
        return tuple(send(ty.at[ps, k, pl.ds(2, 2)], ry1.at[ps, k], 2, s_y1.at[j, k], to)
                     for k, to in enumerate((dev_yn, dev_yf)))

    def y2(j):
        ps = pl.ds(*y_jobs[j])
        return tuple(send(ty.at[ps, k, 1], ry2.at[ps, k], 3, s_y2.at[j, k], to)
                     for k, to in enumerate((dev_yf, dev_yn)))

    def y3(j):
        ps = pl.ds(*y_jobs[j])
        return send(ty.at[ps, 1, 0], ry3.at[ps], 4, s_y3.at[j], dev_zn)

    def y4(j):
        ps = pl.ds(*y_jobs[j])
        return send(ty.at[ps, 0, 0, 1], ry4.at[ps], 5, s_y4.at[j], dev_zf)

    def y_compute(p, n):
        def store(q, k, zr, yy, rows):
            second = lax.div(zr, 2)
            yr = jnp.where(second == 0, place_a[yy], place_b[yy])
            ty[p + q, second, yr, lax.rem(zr, 2), :, k * LANES:(k + 1) * LANES] = rows

        compute(p, n, store)

    def y_stage0(j):
        for cp in y1(j):
            cp.start()

    def y_stage1(j):
        ps = pl.ds(*y_jobs[j])
        first, second = y1(j), y2(j)
        for k in range(2):
            first[k].wait_recv()
            ty[ps, k, 1] = ty[ps, k, 1] + ry1[ps, k, 1]
            second[k].start()
        for k in range(2):
            ty[ps, k, 0] = ty[ps, k, 0] + ry1[ps, k, 0]

    def y_stage2(j):
        ps = pl.ds(*y_jobs[j])
        a, b = y2(j)
        b.wait_recv()
        ty[ps, 1, 0] = ty[ps, 1, 0] + ry2[ps, 1]
        y3(j).start()
        a.wait_recv()
        ty[ps, 0, 0] = ty[ps, 0, 0] + ry2[ps, 0]

    def y_stage3(j):
        ps = pl.ds(*y_jobs[j])
        y3(j).wait_recv()
        ty[ps, 0, 0, 1] = ty[ps, 0, 0, 1] + ry3[ps, 1]
        y4(j).start()
        ty[ps, 0, 0, 0] = ty[ps, 0, 0, 0] + ry3[ps, 0]

    def keep_part(p, k, v):
        at = (p % 4 * 2 + k) * 32
        part[p // 4, at:at + 32, :] = clipped(v)

    def y_stage4(j):
        y4(j).wait_recv()
        first, n = y_jobs[j]
        for p in range(first, first + n):
            v = ty[p, 0, 0, 0].astype(f32) + ry4[p].astype(f32)
            for k in range(2):
                keep_part(p, k, v[:, k * LANES:(k + 1) * LANES])

    def zp(j):
        return pl.ds(z_first[j], z_jobs[j][1])

    def z1(j):
        return send(tz.at[zp(j), pl.ds(2, 2)], rz1.at[zp(j)], 6, s_z1.at[j], dev_zn)

    def z2(j):
        return send(tz.at[zp(j), 1], rz2.at[zp(j)], 7, s_z2.at[j], dev_zf)

    def z3(j):
        return tuple(send(tz.at[zp(j), 0, k, pl.ds(2, 2)], rz3.at[zp(j), k], 8, s_z3.at[j, k], to)
                     for k, to in enumerate((dev_yn, dev_yf)))

    def z4(j):
        return tuple(send(tz.at[zp(j), 0, k, 1], rz4.at[zp(j), k], 9, s_z4.at[j, k], to)
                     for k, to in enumerate((dev_yf, dev_yn)))

    def z_compute(m, p, n):
        def store(q, k, zr, yy, rows):
            tz[m + q, zr, k, (place_a, place_b)[k][yy]] = rows

        compute(p, n, store)

    def z_stage0(j):
        z1(j).start()

    def z_stage1(j):
        ps = zp(j)
        z1(j).wait_recv()
        tz[ps, 1] = tz[ps, 1] + rz1[ps, 1]
        z2(j).start()
        tz[ps, 0] = tz[ps, 0] + rz1[ps, 0]

    def z_stage2(j):
        ps = zp(j)
        z2(j).wait_recv()
        tz[ps, 0] = tz[ps, 0] + rz2[ps]
        for cp in z3(j):
            cp.start()

    def z_stage3(j):
        ps = zp(j)
        first, second = z3(j), z4(j)
        for k in range(2):
            first[k].wait_recv()
            tz[ps, 0, k, 1] = tz[ps, 0, k, 1] + rz3[ps, k, 1]
            second[k].start()
        for k in range(2):
            tz[ps, 0, k, 0] = tz[ps, 0, k, 0] + rz3[ps, k, 0]

    def z_stage4(j):
        for k, cp in enumerate(z4(j)):
            cp.wait_recv()
            for q in range(z_jobs[j][1]):
                m = z_first[j] + q
                keep_part(z_jobs[j][0] + q, k, tz[m, 0, k, 0].astype(f32) + rz4[m, k].astype(f32))

    def x_copies(g):
        return [send(coded_x.at[g, x_to[d]], got_x.at[g, d], 10, s_x.at[g], dev_x[d]) for d in range(3)]

    def h_copies(g):
        return [send(coded_h.at[g, h_to[d][0] * 2 + h_to[d][1]], got_h.at[g, d], 11, s_h.at[g], dev_h[d])
                for d in range(3)]

    def send_x(g):
        for d in range(16):
            rows = [part[g, pl.ds(2 * d + e, 8, stride=32), :] for e in range(2)]
            coded_x[g, (d % 8) // 2, d // 8, d % 2] = jnp.concatenate(rows, axis=0).astype(bf16)
        for cp in x_copies(g):
            cp.start()

    def sum_x(g):
        pltpu.make_async_copy(got_x.at[g], got_x.at[g], s_x.at[g]).wait()
        total = coded_x[g, x].astype(f32)
        for d in range(3):
            total = total + got_x[g, d].astype(f32)
        coded_h[g] = total.astype(bf16).reshape(4, 16, LANES)
        for cp in h_copies(g):
            cp.start()

    def finish(g):
        pltpu.make_async_copy(got_h.at[g], got_h.at[g], s_h.at[g]).wait()
        for half, a, b in ((c, coded_h[g, c * 2 + h], got_h[g, 0]), (1 - c, got_h[g, 1], got_h[g, 2])):
            total = a.astype(f32) + b.astype(f32)
            hi = total.astype(bf16)
            rest = (total - hi.astype(f32)).astype(bf16)
            r = h2[0:LANES, 0:LANES]
            v = jnp.dot(hi, r, preferred_element_type=f32) + jnp.dot(rest, r, preferred_element_type=f32)
            v = v * (1.0 / LANES)
            to = pl.ds(pl.multiple_of(half * (2 * pairs) + g * 8, 8), 8)
            out[0, to, :] = v[0:8]
            out[1, to, :] = v[8:16]

    run = (y_stage0, y_stage1, y_stage2, y_stage3, y_stage4, z_stage0, z_stage1, z_stage2, z_stage3, z_stage4,
           send_x, sum_x, finish)
    starts = [k for k, (stage, _) in enumerate(steps) if stage in (Y0, Z0)] + [len(steps)]
    assert starts[0] == 0
    turns = len(starts) - 1
    sort = [(0 if steps[k][0] == Y0 else 2) + (2 - n) for k, (_, n) in zip(starts, first_use)]
    place_of = [z_first[steps[k][1]] if steps[k][0] == Z0 else 0 for k in starts[:-1]]

    def pick(t, values):
        at = jnp.int32(values[0])
        for k, v in enumerate(values):
            if v != values[0]:
                at = jnp.where(t == k, v, at)
        return at

    def inputs(k):
        load(*first_use[k]).wait()
        lend(*first_use[k]).wait_recv()

    def turn_of(t):
        first, now, m = pick(t, [p for p, _ in first_use]), pick(t, sort), pick(t, place_of)
        for kind in sorted(set(sort)):
            @pl.when(now == kind)
            def _():
                if kind < 2:
                    y_compute(first, 2 - kind)
                else:
                    z_compute(m, first, 4 - kind)

        def among(a, b):
            if b - a > 1:
                mid = (a + b) // 2
                pl.when(t < mid)(lambda: among(a, mid))
                pl.when(t >= mid)(lambda: among(mid, b))
                return
            for stage, j in steps[starts[a]:starts[b]]:
                run[stage](j)
            if b < turns:
                inputs(b)

        among(0, turns)

    inputs(0)
    each(turns, turn_of)

    once = [(0, c_sib), (1, asib), (6, tz.at[:, pl.ds(2, 2)]), (7, tz.at[:, 1]), (8, tz.at[:, 0, :, pl.ds(2, 2)]),
            (9, tz.at[:, 0, :, 1]), (10, coded_x.at[:, pl.ds(0, 3)]), (11, coded_h.at[:, pl.ds(0, 3)])]
    ny = sum(n for _, n in y_jobs)
    once += [(2, ty.at[0:ny, :, pl.ds(2, 2)]), (3, ty.at[0:ny, :, 1]), (4, ty.at[0:ny, 1, 0]),
             (5, ty.at[0:ny, 0, 0, 1])]
    for kind, ref in once:
        pltpu.make_async_copy(ref, ref, s_send.at[kind]).wait()


def on_device(activations, cotangent):
    dma = pltpu.SemaphoreType.DMA
    vm = pltpu.VMEM
    ny, nz = len(y_jobs), len(z_jobs)
    nzp = sum(n for _, n in z_jobs)
    out = pl.pallas_call(
        kernel,
        out_shape=jax.ShapeDtypeStruct((2, 4 * pairs, LANES), f32),
        in_specs=[pl.BlockSpec(memory_space=pltpu.HBM)] * 2,
        out_specs=pl.BlockSpec(memory_space=pltpu.VMEM),
        scratch_shapes=[
            vm((256, 256), bf16),
            vm((2, ROWS, 2 * TOK), bf16),
            vm((TOK, ROWS), bf16), vm((TOK, ROWS), bf16),
            vm((TOK, half_cols), bf16), vm((TOK, half_cols), bf16),
            vm((2, 2, 2 * TOK, 256), bf16),
            vm((pairs, 2, 4, 2, 32, 256), bf16),
            vm((nzp, 4, 2, 4, 32, LANES), bf16),
            vm((pairs, 2, 2, 2, 32, 256), bf16), vm((pairs, 2, 2, 32, 256), bf16),
            vm((pairs, 2, 32, 256), bf16), vm((pairs, 32, 256), bf16),
            vm((nzp, 2, 2, 4, 32, LANES), bf16), vm((nzp, 2, 4, 32, LANES), bf16),
            vm((nzp, 2, 2, 32, LANES), bf16), vm((nzp, 2, 32, LANES), bf16),
            vm((rounds, 256, LANES), f32),
            vm((rounds, 4, 2, 2, 16, LANES), bf16), vm((rounds, 3, 2, 2, 16, LANES), bf16),
            vm((rounds, 4, 16, LANES), bf16), vm((rounds, 3, 16, LANES), bf16),
            dma((pairs,)), dma, dma((12,)), dma((1,)), dma((pairs,)),
            dma((ny, 2)), dma((ny, 2)), dma((ny,)), dma((ny,)),
            dma((nz,)), dma((nz,)), dma((nz, 2)), dma((nz, 2)),
            dma((rounds,)), dma((rounds,)),
        ],
        compiler_params=pltpu.CompilerParams(
            collective_id=0, has_side_effects=True, vmem_limit_bytes=64 * 1024 * 1024 - 10560 * 1024),
        name="reduce_gradient",
    )(activations, cotangent)
    return out.reshape(2, 2 * half_cols)


def solution(mesh):
    placed = (P(("inner", "outer"), None), P(("inner", "outer"), None))
    return jax.shard_map(
        on_device,
        mesh=mesh,
        in_specs=placed,
        out_specs=P(("inner", "outer"), None),
        check_vma=False,
    )
```
